32 devices in a mesh: gene: 8 (over y, x, core), samp: 4 (over z).
Axes of the slice: x: 2, y: 2, z: 4, core: 2. Of those that a mesh axis runs over, the one named last changes fastest.
Arguments:
- dosage: bfloat16 [6144, 5120], P('gene', 'samp'), may hold values from 0 to 2
- expression: float32 [5120, 16], P('samp', 'gene'), may hold values from -6 to 6
- perms: int32 [128, 5120], P(None, 'samp'), may hold values from 0 to 5119, each once within a row
- windows: int32 [16, 2], P('gene'), may hold values from 0 to 6144, as said below
- order: int32 [16], replicated, may hold values from 0 to 15, each once
Outputs:
- observed: float32 [16], P('gene')
- successive: float32 [16, 128], P('gene')
The draws below stay inside these ranges and needn't reach their ends.
Inputs may be any that keep to these rules, and one draw needn't show every extreme that they name: `windows`: gene i's window [start, end) starts within the 768 variants before the block of variants i // 2 * 768 to (i // 2 + 1) * 768 - 1, or at 0, and ends within the 768 variants after that block, or at 6144; start < end.
All inputs are finite; a program needn't handle non-finite values.
Results may differ from the reference program's by a relative error of at most 0.0015.
Values may be sent and summed in bfloat16 or wider, within the bound.
A program may use at most 128 MiB of HBM per device.

```python
import jax
import jax.numpy as jnp
from jax import lax

VAR_DEV = 768
GENE_DEV = 2
PERMS = 128
GENES = 16
VARIANTS = 6144
SAMPLES = 5120
N_GENE = 8


def draw_windows(key, part):
    left_key = jax.random.fold_in(key, 11)
    right_key = jax.random.fold_in(key, 23)
    owner = jnp.arange(GENES, dtype=jnp.int32) // GENE_DEV
    before = jax.random.randint(left_key, (GENES,), 1, VAR_DEV + 1, dtype=jnp.int32)
    after = jax.random.randint(right_key, (GENES,), 1, VAR_DEV + 1, dtype=jnp.int32)
    start = jnp.maximum(owner * VAR_DEV - before, 0)
    finish = jnp.minimum((owner + 1) * VAR_DEV + after, VARIANTS)
    return jnp.stack([start, finish], axis=1).astype(jnp.int32)


def block_scale(own_key, shape, cuts, least, largest):
    def one(position, blocks):
        heights = jax.random.uniform(jax.random.fold_in(jax.random.fold_in(own_key, 6), position), (blocks,), jnp.float32, least / len(cuts), largest / len(cuts))
        return jnp.repeat(jnp.exp(heights), shape[position] // blocks).reshape((-1,) + (1,) * (len(shape) - position - 1))

    factor_of = one(*cuts[0])
    for cut in cuts[1:]:
        factor_of = factor_of * one(*cut)
    return factor_of


def normal_values(rng, shape, width, bound, shards=(), kind=jnp.bfloat16):
    drawn = width * jax.random.normal(rng, shape, jnp.float32)
    if shards:
        drawn = drawn * block_scale(rng, shape, shards, -0.22, 0.18)
    return jnp.clip(drawn, -bound, bound).astype(kind)


def setup_inputs(seed: int = 0) -> dict:
    arg_keys = jax.random.split(jax.random.key(seed), 6)
    dosage = jnp.clip(2.0 * jax.random.uniform(arg_keys[0], (VARIANTS, SAMPLES), jnp.float32) ** block_scale(arg_keys[0], (VARIANTS, SAMPLES), ((0, 8), (1, 4)), -0.2, 0.2), 0.0, 2.0).astype(jnp.bfloat16)
    expression = normal_values(arg_keys[1], (SAMPLES, GENES), 1.0, 6.0, ((0, 4), (1, 8)), jnp.float32)
    perms = jax.vmap(lambda own: jax.random.permutation(own, SAMPLES))(jax.random.split(arg_keys[2], PERMS)).reshape((PERMS, SAMPLES)).astype(jnp.int32)
    windows = draw_windows(jax.random.fold_in(arg_keys[5], 71), 0)
    order = jax.random.permutation(arg_keys[4], GENES).astype(jnp.int32)
    return {"dosage": dosage, "expression": expression, "perms": perms, "windows": windows, "order": order}


epsilon = 1e-06

def reference(dosage, expression, perms, windows, order):
    samples = expression.shape[0]
    center = expression - lax.optimization_barrier(jnp.mean(expression, axis=0, keepdims=True))
    scaled = center * lax.rsqrt(lax.optimization_barrier(jnp.mean(center * center, axis=0, keepdims=True)) + epsilon)
    standard = scaled.astype(jnp.bfloat16)
    padded = jnp.pad(dosage, ((VAR_DEV, VAR_DEV), (0, 0)))
    totals = lax.optimization_barrier(jnp.sum(padded.astype(jnp.float32), axis=1))
    squares = lax.optimization_barrier(jnp.sum(jnp.square(padded.astype(jnp.float32)), axis=1))
    row_mean = totals / samples
    row_var = squares / samples - row_mean * row_mean + epsilon
    factor = lax.rsqrt(row_var * samples)

    def one_owner(owner):
        first = owner * VAR_DEV
        block_rows = lax.dynamic_slice_in_dim(padded, first, 3 * VAR_DEV, 0)
        row_scale = lax.dynamic_slice_in_dim(factor, first, 3 * VAR_DEV, 0)
        columns = lax.dynamic_slice_in_dim(standard, (owner * GENE_DEV).astype(jnp.int32), GENE_DEV, 1)
        shuffled = jnp.transpose(columns[perms], (1, 2, 0)).reshape(samples, GENE_DEV * PERMS)
        partial_value = jnp.dot(block_rows, shuffled, preferred_element_type=jnp.float32)
        direct = jnp.dot(block_rows, columns, preferred_element_type=jnp.float32)
        row_index = (first - VAR_DEV + jnp.arange(3 * VAR_DEV, dtype=jnp.int32)).astype(jnp.int32)
        bounds = lax.dynamic_slice_in_dim(windows, (owner * GENE_DEV).astype(jnp.int32), GENE_DEV, 0)
        inside = (row_index[:, None] >= bounds[None, :, 0]) & (row_index[:, None] < bounds[None, :, 1])
        values = jnp.abs(partial_value).reshape(3 * VAR_DEV, GENE_DEV, PERMS) * row_scale[:, None, None]
        maxima = lax.optimization_barrier(jnp.max(jnp.where(inside[:, :, None], values, jnp.float32(0.0)), axis=0))
        seen = lax.optimization_barrier(jnp.max(jnp.where(inside, jnp.abs(direct) * row_scale[:, None], jnp.float32(0.0)), axis=0))
        return (seen, maxima)
    seen, maxima = lax.map(one_owner, jnp.arange(N_GENE, dtype=jnp.int32))
    observed = seen.reshape(GENES)
    ranked = maxima.reshape(GENES, PERMS)[order]
    successive = lax.cummax(ranked, axis=0, reverse=True)
    return (observed, successive)
```

```python
import jax
import jax.numpy as jnp
from jax import lax
from jax.sharding import PartitionSpec as P

epsilon = 1e-06


def padded(block, sides, width):
    for axis, dim in sides:
        count = lax.axis_size(axis)
        forward = [(i, i + 1) for i in range(count - 1)]
        backward = [(target, source) for source, target in forward]
        low = lax.ppermute(
            lax.slice_in_dim(block, block.shape[dim] - width, None, axis=dim), axis, forward
        )
        high = lax.ppermute(lax.slice_in_dim(block, 0, width, axis=dim), axis, backward)
        block = jnp.concatenate([low, block, high], axis=dim)
    return block


def prefix(shard, axis, combine, identity):
    size, index = (lax.axis_size(axis), lax.axis_index(axis))
    everything = lax.all_gather(shard, axis)
    start = jnp.broadcast_to(jnp.asarray(identity, shard.dtype), shard.shape)

    def hop(k, before):
        at = size - 1 - k
        reached = at > index
        new = combine(before, everything[at])
        return jnp.where(reached, new, before)

    return lax.fori_loop(0, size, hop, start)


def permute_rows(wide, perms):
    permutations, samp_dev = perms.shape
    gene_cols = wide.shape[1]
    picked = jnp.take(wide, perms, axis=0)
    return jnp.transpose(picked, (1, 2, 0)).reshape(samp_dev, gene_cols * permutations)


def pick_rows(index, table):
    choose = (index[:, None] == jnp.arange(table.shape[0], dtype=jnp.int32)[None, :]).astype(
        jnp.float32
    )
    return jnp.dot(
        choose, table, precision=lax.Precision.HIGHEST, preferred_element_type=jnp.float32
    )


def on_device(dosage, expression, perms, windows, order):
    var_dev, samp_dev = dosage.shape
    gene_dev = expression.shape[1]
    permutations = perms.shape[0]
    samples = samp_dev * lax.axis_size("samp")
    gene_place = lax.axis_index("gene")
    samp_place = lax.axis_index("samp")
    every_sample = lax.all_gather(expression, "samp", axis=0, tiled=True)
    center = every_sample - jnp.mean(every_sample, axis=0, keepdims=True)
    scaled = center * lax.rsqrt(jnp.mean(center * center, axis=0, keepdims=True) + epsilon)
    standard = scaled.astype(jnp.bfloat16)
    wide = padded(standard, (("gene", 1),), gene_dev)
    bounds = padded(windows, (("gene", 0),), gene_dev)
    row_index = gene_place * var_dev + jnp.arange(var_dev, dtype=jnp.int32)
    gene_cols = wide.shape[1]
    columns = lax.dynamic_slice_in_dim(wide, samp_place * samp_dev, samp_dev, 0)
    shuffled = permute_rows(wide, perms)
    totals = jnp.sum(dosage.astype(jnp.float32), axis=1)
    squares = jnp.sum(jnp.square(dosage.astype(jnp.float32)), axis=1)
    direct = jnp.dot(dosage, columns, preferred_element_type=jnp.float32)
    partial_value = jnp.dot(dosage, shuffled, preferred_element_type=jnp.float32)
    partial_value, direct, totals, squares = lax.psum(
        (partial_value, direct, totals, squares), "samp"
    )
    row_mean = totals / samples
    row_var = squares / samples - row_mean * row_mean + epsilon
    row_scale = lax.rsqrt(row_var * samples)
    inside = (row_index[:, None] >= bounds[None, :, 0]) & (row_index[:, None] < bounds[None, :, 1])
    values = (
        jnp.abs(partial_value).reshape(partial_value.shape[0], gene_cols, permutations)
        * row_scale[:, None, None]
    )
    maxima = jnp.max(jnp.where(inside[:, :, None], values, jnp.float32(0.0)), axis=0)
    observed = jnp.max(
        jnp.where(inside, jnp.abs(direct) * row_scale[:, None], jnp.float32(0.0)), axis=0
    )
    width = gene_dev * permutations
    left_part = jnp.concatenate([maxima[:gene_dev].reshape(width), observed[:gene_dev]])
    right_part = jnp.concatenate([maxima[2 * gene_dev :].reshape(width), observed[2 * gene_dev :]])
    packed = jnp.stack([left_part, right_part], axis=0)
    arrived = padded(packed, (("gene", 0),), 1)
    from_left = arrived[0]
    from_right = arrived[3]
    maxima = jnp.maximum(
        maxima[gene_dev : 2 * gene_dev],
        jnp.maximum(from_left[:width], from_right[:width]).reshape(gene_dev, permutations),
    )
    observed = jnp.maximum(
        observed[gene_dev : 2 * gene_dev], jnp.maximum(from_left[width:], from_right[width:])
    )
    everyone = lax.all_gather(maxima, "gene", axis=0, tiled=True)
    my_genes = lax.dynamic_slice_in_dim(order, gene_place * gene_dev, gene_dev, 0)
    my_rows = pick_rows(my_genes, everyone)
    suffix_rows = [my_rows[gene_dev - 1]]
    for k in range(gene_dev - 2, -1, -1):
        suffix_rows.insert(0, jnp.maximum(my_rows[k], suffix_rows[0]))
    local_suffix = jnp.stack(suffix_rows, axis=0)
    later = prefix(local_suffix[0], "gene", jnp.maximum, jnp.zeros((permutations,), jnp.float32))
    successive = jnp.maximum(local_suffix, later[None, :])
    return (observed, successive)


def solution(mesh):
    placed = (P("gene", "samp"), P("samp", "gene"), P(None, "samp"), P("gene", None), P())
    return jax.shard_map(
        on_device,
        mesh=mesh,
        in_specs=placed,
        out_specs=(P("gene"), P("gene", None)),
        check_vma=False,
    )
```

```python
import jax
import jax.numpy as jnp
from jax import lax
from jax.experimental import pallas as pl
from jax.experimental.pallas import tpu as pltpu
from jax.sharding import PartitionSpec as P

epsilon = 1e-06


def padded(block, sides, width):
    for axis, dim in sides:
        count = lax.axis_size(axis)
        forward = [(i, i + 1) for i in range(count - 1)]
        backward = [(target, source) for source, target in forward]
        low = lax.ppermute(
            lax.slice_in_dim(block, block.shape[dim] - width, None, axis=dim), axis, forward
        )
        high = lax.ppermute(lax.slice_in_dim(block, 0, width, axis=dim), axis, backward)
        block = jnp.concatenate([low, block, high], axis=dim)
    return block


def prefix(shard, axis, combine, identity):
    size, index = (lax.axis_size(axis), lax.axis_index(axis))
    everything = lax.all_gather(shard, axis)
    start = jnp.broadcast_to(jnp.asarray(identity, shard.dtype), shard.shape)

    def hop(k, before):
        at = size - 1 - k
        reached = at > index
        new = combine(before, everything[at])
        return jnp.where(reached, new, before)

    return lax.fori_loop(0, size, hop, start)


LANES = 128


def encode(standard):
    value = standard.astype(jnp.float32)
    size = jnp.abs(value)
    down = jnp.zeros(value.shape, jnp.int32)
    for step in (64, 32, 16, 8, 4, 2, 1):
        small = size < 2.0 ** (7 - step)
        size = jnp.where(small, size * 2.0**step, size)
        down = down + jnp.where(small, step, 0)
    mantissa = jnp.where(value < 0, -2.0 * size, 2.0 * size).astype(jnp.int32)
    return down * 512 + mantissa + 256


def pack_codes(wide):
    codes = encode(wide).T
    words = codes[0::2] + (codes[1::2] << 16)
    return words.reshape(words.shape[0], -1, LANES)


def powers():
    lane = lax.broadcasted_iota(jnp.int32, (16, LANES), 1)
    power = jnp.full((16, LANES), 0.5, jnp.float32)
    for step in (64, 32, 16, 8, 4, 2, 1):
        power = jnp.where((lane & step) != 0, power * 2.0**-step, power)
    return jnp.where(lane >= 126, 0.0, power)


def pick(table, index):
    return jnp.take_along_axis(table, index, axis=1)


def shuffle_tile(table_ref, index, words, rows):
    low = index & (LANES - 1)
    high = index >> 7
    shape = index.shape
    found = [jnp.zeros(shape, jnp.int32) for _ in range(words)]
    for row in range(rows):
        here = high == row
        for word in range(words):
            entry = jnp.broadcast_to(table_ref[word, pl.ds(row, 1), :], shape)
            found[word] = jnp.where(here, pick(entry, low), found[word])
    return found


def decode(code, power):
    mantissa = ((code & 511) - 256).astype(jnp.float32)
    return (mantissa * pick(power, (code >> 9) & 127)).astype(jnp.bfloat16)


def shuffle_kernel(table_ref, perms_ref, out_ref):
    words, rows, _ = table_ref.shape
    permutations, samp_dev = perms_ref.shape
    power = powers()
    across = samp_dev // LANES

    def tile(t, carry):
        p = pl.multiple_of((t // across) * 16, 16)
        s = pl.multiple_of((t % across) * LANES, LANES)
        index = perms_ref[pl.ds(p, 16), pl.ds(s, LANES)]
        found = shuffle_tile(table_ref, index, words, rows)
        for word in range(words):
            out_ref[2 * word, pl.ds(p, 16), pl.ds(s, LANES)] = decode(found[word], power)
            out_ref[2 * word + 1, pl.ds(p, 16), pl.ds(s, LANES)] = decode(
                found[word] >> 16, power
            )
        return carry

    lax.fori_loop(0, permutations // 16 * across, tile, 0)


def permute_rows(wide, perms):
    permutations, samp_dev = perms.shape
    genes = wide.shape[1]
    out = pl.pallas_call(
        shuffle_kernel,
        out_shape=jax.ShapeDtypeStruct((genes, permutations, samp_dev), jnp.bfloat16),
        in_specs=[pl.BlockSpec(memory_space=pltpu.VMEM)] * 2,
        out_specs=pl.BlockSpec(memory_space=pltpu.VMEM),
        compiler_params=pltpu.CompilerParams(vmem_limit_bytes=32 * 2**20),
    )(pack_codes(wide), perms)
    return out.reshape(genes * permutations, samp_dev)


def pick_rows(index, table):
    choose = (index[:, None] == jnp.arange(table.shape[0], dtype=jnp.int32)[None, :]).astype(
        jnp.float32
    )
    return jnp.dot(
        choose, table, precision=lax.Precision.HIGHEST, preferred_element_type=jnp.float32
    )


def on_device(dosage, expression, perms, windows, order):
    var_dev, samp_dev = dosage.shape
    gene_dev = expression.shape[1]
    permutations = perms.shape[0]
    samples = samp_dev * lax.axis_size("samp")
    gene_place = lax.axis_index("gene")
    samp_place = lax.axis_index("samp")
    every_sample = lax.all_gather(expression, "samp", axis=0, tiled=True)
    center = every_sample - jnp.mean(every_sample, axis=0, keepdims=True)
    scaled = center * lax.rsqrt(jnp.mean(center * center, axis=0, keepdims=True) + epsilon)
    standard = scaled.astype(jnp.bfloat16)
    wide = padded(standard, (("gene", 1),), gene_dev)
    bounds = padded(windows, (("gene", 0),), gene_dev)
    row_index = gene_place * var_dev + jnp.arange(var_dev, dtype=jnp.int32)
    gene_cols = wide.shape[1]
    columns = lax.dynamic_slice_in_dim(wide, samp_place * samp_dev, samp_dev, 0)
    shuffled = permute_rows(wide, perms)
    totals = jnp.sum(dosage.astype(jnp.float32), axis=1)
    squares = jnp.sum(jnp.square(dosage.astype(jnp.float32)), axis=1)
    direct = jnp.dot(dosage, columns, preferred_element_type=jnp.float32)
    partial_value = lax.dot_general(
        dosage, shuffled, (((1,), (1,)), ((), ())), preferred_element_type=jnp.float32
    )
    partial_value, direct, totals, squares = lax.psum(
        (partial_value, direct, totals, squares), "samp"
    )
    row_mean = totals / samples
    row_var = squares / samples - row_mean * row_mean + epsilon
    row_scale = lax.rsqrt(row_var * samples)
    inside = (row_index[:, None] >= bounds[None, :, 0]) & (row_index[:, None] < bounds[None, :, 1])
    values = (
        jnp.abs(partial_value).reshape(partial_value.shape[0], gene_cols, permutations)
        * row_scale[:, None, None]
    )
    maxima = jnp.max(jnp.where(inside[:, :, None], values, jnp.float32(0.0)), axis=0)
    observed = jnp.max(
        jnp.where(inside, jnp.abs(direct) * row_scale[:, None], jnp.float32(0.0)), axis=0
    )
    width = gene_dev * permutations
    left_part = jnp.concatenate([maxima[:gene_dev].reshape(width), observed[:gene_dev]])
    right_part = jnp.concatenate([maxima[2 * gene_dev :].reshape(width), observed[2 * gene_dev :]])
    packed = jnp.stack([left_part, right_part], axis=0)
    arrived = padded(packed, (("gene", 0),), 1)
    from_left = arrived[0]
    from_right = arrived[3]
    maxima = jnp.maximum(
        maxima[gene_dev : 2 * gene_dev],
        jnp.maximum(from_left[:width], from_right[:width]).reshape(gene_dev, permutations),
    )
    observed = jnp.maximum(
        observed[gene_dev : 2 * gene_dev], jnp.maximum(from_left[width:], from_right[width:])
    )
    everyone = lax.all_gather(maxima, "gene", axis=0, tiled=True)
    my_genes = lax.dynamic_slice_in_dim(order, gene_place * gene_dev, gene_dev, 0)
    my_rows = pick_rows(my_genes, everyone)
    suffix_rows = [my_rows[gene_dev - 1]]
    for k in range(gene_dev - 2, -1, -1):
        suffix_rows.insert(0, jnp.maximum(my_rows[k], suffix_rows[0]))
    local_suffix = jnp.stack(suffix_rows, axis=0)
    later = prefix(local_suffix[0], "gene", jnp.maximum, jnp.zeros((permutations,), jnp.float32))
    successive = jnp.maximum(local_suffix, later[None, :])
    return (observed, successive)


def solution(mesh):
    placed = (P("gene", "samp"), P("samp", "gene"), P(None, "samp"), P("gene", None), P())
    return jax.shard_map(
        on_device,
        mesh=mesh,
        in_specs=placed,
        out_specs=(P("gene"), P("gene", None)),
        check_vma=False,
    )
```

```python
import functools

import jax
import jax.numpy as jnp
from jax import lax
from jax.experimental import pallas as pl
from jax.experimental.pallas import tpu as pltpu
from jax.sharding import PartitionSpec as P

epsilon = 1e-06


LANES = 128


def encode(value):
    size = jnp.abs(value)
    down = jnp.zeros(value.shape, jnp.int32)
    for step in (64, 32, 16, 8, 4, 2, 1):
        small = size < 2.0 ** (7 - step)
        size = jnp.where(small, size * 2.0**step, size)
        down = down + jnp.where(small, step, 0)
    mantissa = jnp.where(value < 0, -2.0 * size, 2.0 * size).astype(jnp.int32)
    return down * 512 + mantissa + 256


def powers():
    lane = lax.broadcasted_iota(jnp.int32, (16, LANES), 1)
    power = jnp.full((16, LANES), 0.5, jnp.float32)
    for step in (64, 32, 16, 8, 4, 2, 1):
        power = jnp.where((lane & step) != 0, power * 2.0**-step, power)
    return jnp.where(lane >= 126, 0.0, power)


def pick(table, index):
    return jnp.take_along_axis(table, index, axis=1)


def decode(code, power):
    mantissa = ((code & 511) - 256).astype(jnp.float32)
    return (mantissa * pick(power, (code >> 9) & 127)).astype(jnp.bfloat16)


def rows_dot(left, right):
    return lax.dot_general(left, right, (((1,), (1,)), ((), ())), preferred_element_type=jnp.float32)


def whole_sum(block):
    return jnp.sum(jnp.sum(block, axis=0, keepdims=True), axis=1, keepdims=True)


def scan_kernel(
    gene_size,
    samp_size,
    samples,
    message_ref,
    dosage_ref,
    perms_ref,
    out_ref,
    arrived,
    table,
    alone,
    moments,
    directs,
    shuffled,
    mine,
    outgoing,
    incoming,
    peaks,
    rows_z,
    message_send,
    message_recv,
    moment_send,
    moment_recv,
    direct_send,
    direct_recv,
    block_send,
    block_recv,
    row_send,
    row_recv,
    all_send,
    all_recv,
):
    var_dev, samp_dev = dosage_ref.shape
    permutations = perms_ref.shape[0]
    gene_dev = message_ref.shape[0]
    genes = 3 * gene_dev
    share = permutations // samp_size
    across = samp_dev // LANES
    g = lax.axis_index("gene")
    z = lax.axis_index("samp")

    def there(dg, dz):
        return {
            "gene": lax.rem(g + dg + gene_size, gene_size),
            "samp": lax.rem(z + dz, samp_size),
        }

    def send(source, target, send_sem, recv_sem, device):
        return pltpu.make_async_remote_copy(
            src_ref=source,
            dst_ref=target,
            send_sem=send_sem,
            recv_sem=recv_sem,
            device_id=device,
            device_id_type=pl.DeviceIdType.MESH,
        )

    near = [(dg, dz) for dz in range(samp_size) for dg in (-1, 0, 1) if (dg, dz) != (0, 0)]
    far = [(dg, 0) for dg in range(2, gene_size - 1)]
    barrier = pltpu.get_barrier_semaphore()
    for dg, dz in near + far:
        pl.semaphore_signal(
            barrier, inc=1, device_id=there(dg, dz), device_id_type=pl.DeviceIdType.MESH
        )
    pl.semaphore_wait(barrier, len(near + far))

    pending = []
    for dg, dz in near:
        copy = send(
            message_ref,
            arrived.at[1 - dg, z],
            message_send.at[1 - dg, dz],
            message_recv.at[1 - dg, z],
            there(dg, dz),
        )
        copy.start()
        pending.append(copy)
    arrived[1, z] = message_ref[...]

    ones = jnp.ones((16, samp_dev), jnp.bfloat16)
    step = 256 if var_dev % 256 == 0 else var_dev
    for v in range(0, var_dev, step):
        part = dosage_ref[v : v + step, :]
        wide = part.astype(jnp.float32)
        square = wide * wide
        upper = square.astype(jnp.bfloat16)
        lower = (square - upper.astype(jnp.float32)).astype(jnp.bfloat16)
        moments[z, 0:8, v : v + step] = rows_dot(ones, part)[0:8]
        moments[z, 8:16, v : v + step] = (rows_dot(ones, upper) + rows_dot(ones, lower))[0:8]
    for dz in range(1, samp_size):
        copy = send(
            moments.at[z], moments.at[z], moment_send.at[dz], moment_recv.at[z], there(0, dz)
        )
        copy.start()
        pending.append(copy)

    for r in (0, 1, 2):
        for dz in range(samp_size):
            if (r, dz) != (1, 0):
                source = lax.rem(z + dz, samp_size)
                send(
                    message_ref,
                    arrived.at[r, source],
                    message_send.at[r, dz],
                    message_recv.at[r, source],
                    there(0, 1),
                ).wait_recv()

    alone[...] = jnp.zeros_like(alone)
    sums = []
    for r in range(3):
        for pair in range(gene_dev // 2):
            codes = [[], []]
            for half in range(2):
                j = 2 * pair + half
                blocks = [arrived[r, k, j, 0:across, :] for k in range(samp_size)]
                mean = whole_sum(sum(blocks)) / samples
                spread = whole_sum(sum(jnp.square(k - mean) for k in blocks)) / samples
                factor = lax.rsqrt(spread + epsilon)
                total = jnp.zeros((across, LANES), jnp.float32)
                for k in range(samp_size):
                    value = ((blocks[k] - mean) * factor).astype(jnp.bfloat16).astype(jnp.float32)
                    total = total + value
                    codes[half].append(encode(value))
                sums.append(whole_sum(total))
                own = (arrived[r, z, j, 0:across, :] - mean) * factor
                own = own.astype(jnp.bfloat16).astype(jnp.float32)
                row = r * gene_dev + j
                for h in range(across):
                    alone[row : row + 1, h * LANES : (h + 1) * LANES] = own[h : h + 1, :]
            word = r * (gene_dev // 2) + pair
            for k in range(samp_size):
                table[word, k, 0:across, :] = codes[0][k] + (codes[1][k] << 16)

    each = alone[...].astype(jnp.bfloat16)
    for v in range(0, var_dev, step):
        directs[z, :, v : v + step] = rows_dot(each, dosage_ref[v : v + step, :])
    for dz in range(1, samp_size):
        copy = send(
            directs.at[z], directs.at[z], direct_send.at[dz], direct_recv.at[z], there(0, dz)
        )
        copy.start()
        pending.append(copy)

    for dz in range(1, samp_size):
        source = lax.rem(z + dz, samp_size)
        send(
            moments.at[z],
            moments.at[source],
            moment_send.at[dz],
            moment_recv.at[source],
            there(0, dz),
        ).wait_recv()
    totals = sum(moments[k, 0:1, :] for k in range(samp_size))
    squares = sum(moments[k, 8:9, :] for k in range(samp_size))
    row_mean = totals / samples
    row_scale = lax.rsqrt((squares / samples - row_mean * row_mean + epsilon) * samples)

    power = powers()
    words = table.shape[0]

    def block(target):
        first = pl.multiple_of(target * share, share)

        def tile(t, carry):
            p = pl.multiple_of((t // across) * 16, 16)
            s = pl.multiple_of((t % across) * LANES, LANES)
            index = perms_ref[pl.ds(pl.multiple_of(first + p, 16), 16), pl.ds(s, LANES)]
            low = index & (LANES - 1)
            high = index >> 7
            found = [jnp.zeros(index.shape, jnp.int32) for _ in range(words)]
            for k in range(samp_size):
                for h in range(across):
                    here = high == k * across + h
                    for w in range(words):
                        entry = jnp.broadcast_to(table[w, k, h : h + 1, :], index.shape)
                        found[w] = jnp.where(here, pick(entry, low), found[w])
            for w in range(words):
                for half in range(2):
                    row = pl.multiple_of((2 * w + half) * share + p, 16)
                    shuffled[pl.ds(row, 16), pl.ds(s, LANES)] = decode(
                        found[w] >> (16 * half), power
                    )
            return carry

        lax.fori_loop(0, share // 16 * across, tile, 0)
        taken = shuffled[...]
        column = jnp.sum(taken.astype(jnp.float32), axis=1, keepdims=True)
        for v in range(0, var_dev, step):
            mine[:, v : v + step] = (
                rows_dot(taken, dosage_ref[v : v + step, :]) - column * row_mean[:, v : v + step]
            )

    def remote(k, carry):
        target = lax.rem(z + 1 + k, samp_size)
        block(target)
        outgoing[k] = mine[...].astype(jnp.bfloat16)
        send(
            outgoing.at[k],
            incoming.at[k],
            block_send.at[k],
            block_recv.at[k],
            {"gene": g, "samp": target},
        ).start()
        return carry

    lax.fori_loop(0, samp_size - 1, remote, 0)
    block(z)

    for dz in range(1, samp_size):
        source = lax.rem(z + dz, samp_size)
        send(
            directs.at[z],
            directs.at[source],
            direct_send.at[dz],
            direct_recv.at[source],
            there(0, dz),
        ).wait_recv()
    direct = sum(directs[k] for k in range(samp_size))
    place = (g * var_dev + lax.broadcasted_iota(jnp.int32, (1, var_dev), 1)).astype(jnp.float32)
    peaks[...] = jnp.zeros_like(peaks)
    for k in range(samp_size - 1):
        send(
            outgoing.at[k], incoming.at[k], block_send.at[k], block_recv.at[k], there(0, k + 1)
        ).wait()

    def fold(values):
        best = values[:, 0:LANES]
        for t in range(LANES, var_dev, LANES):
            best = jnp.maximum(best, values[:, t : t + LANES])
        return best

    for row in range(genes):
        r, j = row // gene_dev, row % gene_dev
        start = arrived[r, 0, j, across : across + 1, 0:1]
        finish = arrived[r, 0, j, across + 1 : across + 2, 0:1]
        weight = jnp.where((place >= start) & (place < finish), row_scale, 0.0)
        rows = slice(row * share, (row + 1) * share)
        total = mine[rows, :] + row_mean * sums[row]
        for k in range(samp_size - 1):
            total = total + incoming[k, rows, :].astype(jnp.float32)
        peaks[rows, :] = fold(jnp.abs(total) * weight)
        last = genes * share + row
        peaks[last : last + 1, :] = fold(jnp.abs(direct[row : row + 1, :]) * weight)
    rows_z[z] = jnp.max(peaks[...].T, axis=0, keepdims=True)
    for dz in range(1, samp_size):
        copy = send(rows_z.at[z], rows_z.at[z], row_send.at[dz], row_recv.at[z], there(0, dz))
        copy.start()
        pending.append(copy)
    for dz in range(1, samp_size):
        source = lax.rem(z + dz, samp_size)
        send(
            rows_z.at[z], rows_z.at[source], row_send.at[dz], row_recv.at[source], there(0, dz)
        ).wait_recv()
    for dg in range(1, gene_size):
        copy = send(rows_z, out_ref.at[g], all_send.at[dg], all_recv.at[g], there(dg, 0))
        copy.start()
        pending.append(copy)
    out_ref[g] = rows_z[...]
    for dg in range(1, gene_size):
        source = lax.rem(g + dg, gene_size)
        send(
            rows_z, out_ref.at[source], all_send.at[dg], all_recv.at[source], there(dg, 0)
        ).wait_recv()
    for copy in pending:
        copy.wait_send()


def up_to(size, unit):
    return -(-size // unit) * unit


def scan(dosage, expression, perms, windows):
    var_dev, samp_dev = dosage.shape
    gene_dev = expression.shape[1]
    permutations = perms.shape[0]
    gene_size, samp_size = lax.axis_size("gene"), lax.axis_size("samp")
    genes = 3 * gene_dev
    across = samp_dev // LANES
    share = permutations // samp_size
    height = up_to(across + 2, 8)
    lines = jnp.concatenate(
        [
            expression.T.reshape(gene_dev, across, LANES),
            jnp.broadcast_to(
                windows.astype(jnp.float32)[:, :, None], (gene_dev, 2, LANES)
            ),
            jnp.zeros((gene_dev, height - across - 2, LANES), jnp.float32),
        ],
        axis=1,
    )
    width = up_to(genes * share + genes, LANES)
    few = up_to(genes, 16)
    dma = pltpu.SemaphoreType.DMA
    kernel = functools.partial(scan_kernel, gene_size, samp_size, samp_dev * samp_size)
    return pl.pallas_call(
        kernel,
        out_shape=jax.ShapeDtypeStruct((gene_size, samp_size, 1, width), jnp.float32),
        in_specs=[pl.BlockSpec(memory_space=pltpu.VMEM)] * 3,
        out_specs=pl.BlockSpec(memory_space=pltpu.VMEM),
        scratch_shapes=[
            pltpu.VMEM((3, samp_size, gene_dev, height, LANES), jnp.float32),
            pltpu.VMEM((genes // 2, samp_size, up_to(across, 8), LANES), jnp.int32),
            pltpu.VMEM((few, samp_dev), jnp.float32),
            pltpu.VMEM((samp_size, 16, var_dev), jnp.float32),
            pltpu.VMEM((samp_size, few, var_dev), jnp.float32),
            pltpu.VMEM((genes * share, samp_dev), jnp.bfloat16),
            pltpu.VMEM((genes * share, var_dev), jnp.float32),
            pltpu.VMEM((samp_size - 1, genes * share, var_dev), jnp.bfloat16),
            pltpu.VMEM((samp_size - 1, genes * share, var_dev), jnp.bfloat16),
            pltpu.VMEM((width, LANES), jnp.float32),
            pltpu.VMEM((samp_size, 1, width), jnp.float32),
            dma((3, samp_size)),
            dma((3, samp_size)),
        ]
        + [dma((samp_size,))] * 8
        + [dma((gene_size,))] * 2,
        compiler_params=pltpu.CompilerParams(
            collective_id=0, has_side_effects=True, vmem_limit_bytes=48 * 2**20
        ),
    )(lines, dosage, perms)


def on_device(dosage, expression, perms, windows, order):
    gene_dev = expression.shape[1]
    permutations = perms.shape[0]
    gene_size, samp_size = lax.axis_size("gene"), lax.axis_size("samp")
    gene_place = lax.axis_index("gene")
    share = permutations // samp_size
    genes = 3 * gene_dev
    found = scan(dosage, expression, perms, windows)[:, :, 0, :]
    maxima = found[:, :, : genes * share].reshape(gene_size, samp_size, 3, gene_dev, share)
    maxima = maxima.transpose(0, 2, 3, 1, 4).reshape(gene_size, 3, gene_dev, permutations)
    seen = found[:, 0, genes * share : genes * share + genes].reshape(gene_size, 3, gene_dev, 1)
    every = jnp.concatenate([maxima, seen], axis=3)
    every = jnp.maximum(
        every[:, 1],
        jnp.maximum(jnp.roll(every[:, 0], -1, axis=0), jnp.roll(every[:, 2], 1, axis=0)),
    )
    observed = lax.dynamic_slice_in_dim(every[:, :, permutations], gene_place, 1, 0)[0]
    ranked = every[:, :, :permutations].reshape(gene_size * gene_dev, permutations)
    ids = jnp.arange(order.shape[0], dtype=jnp.int32)
    rank = jnp.sum(jnp.where(order[None, :] == ids[:, None], ids[None, :], 0), axis=1)
    mine = gene_place * gene_dev + jnp.arange(gene_dev, dtype=jnp.int32)
    later = rank[None, :] >= mine[:, None]
    successive = jnp.max(jnp.where(later[:, :, None], ranked[None], 0.0), axis=1)
    return (observed, successive)


def solution(mesh):
    placed = (P("gene", "samp"), P("samp", "gene"), P(None, "samp"), P("gene", None), P())
    return jax.shard_map(
        on_device,
        mesh=mesh,
        in_specs=placed,
        out_specs=(P("gene"), P("gene", None)),
        check_vma=False,
    )
```

```python
import functools

import jax
import jax.numpy as jnp
from jax import lax
from jax.experimental import pallas as pl
from jax.experimental.pallas import tpu as pltpu
from jax.sharding import PartitionSpec as P

epsilon = 1e-06


LANES = 128


def encode(value):
    size = jnp.abs(value)
    down = jnp.zeros(value.shape, jnp.int32)
    for step in (64, 32, 16, 8, 4, 2, 1):
        small = size < 2.0 ** (7 - step)
        size = jnp.where(small, size * 2.0**step, size)
        down = down + jnp.where(small, step, 0)
    mantissa = jnp.where(value < 0, -2.0 * size, 2.0 * size).astype(jnp.int32)
    return down * 512 + mantissa + 256


def powers():
    lane = lax.broadcasted_iota(jnp.int32, (16, LANES), 1)
    power = jnp.full((16, LANES), 0.5, jnp.float32)
    for step in (64, 32, 16, 8, 4, 2, 1):
        power = jnp.where((lane & step) != 0, power * 2.0**-step, power)
    return jnp.where(lane >= 126, 0.0, power)


def pick(table, index):
    return jnp.take_along_axis(table, index, axis=1)


def decode(code, power):
    mantissa = ((code & 511) - 256).astype(jnp.float32)
    return (mantissa * pick(power, (code >> 9) & 127)).astype(jnp.bfloat16)


def rows_dot(left, right):
    return lax.dot_general(left, right, (((1,), (1,)), ((), ())), preferred_element_type=jnp.float32)


def whole_sum(block):
    return jnp.sum(jnp.sum(block, axis=0, keepdims=True), axis=1, keepdims=True)


def scan_kernel(
    gene_size,
    samp_size,
    samples,
    message_ref,
    dosage_ref,
    perms_ref,
    out_ref,
    arrived,
    table,
    alone,
    moments,
    directs,
    shuffled,
    mine,
    outgoing,
    incoming,
    peaks,
    rows_z,
    message_send,
    message_recv,
    moment_send,
    moment_recv,
    direct_send,
    direct_recv,
    block_send,
    block_recv,
    row_send,
    row_recv,
    all_send,
    all_recv,
    shift_send,
    shift_recv,
):
    var_dev, samp_dev = dosage_ref.shape
    permutations = perms_ref.shape[0]
    gene_dev = message_ref.shape[0]
    genes = 3 * gene_dev
    share = permutations // samp_size
    across = samp_dev // LANES
    g = lax.axis_index("gene")
    z = lax.axis_index("samp")

    def there(dg, dz):
        return {
            "gene": lax.rem(g + dg + gene_size, gene_size),
            "samp": lax.rem(z + dz, samp_size),
        }

    def send(source, target, send_sem, recv_sem, device):
        return pltpu.make_async_remote_copy(
            src_ref=source,
            dst_ref=target,
            send_sem=send_sem,
            recv_sem=recv_sem,
            device_id=device,
            device_id_type=pl.DeviceIdType.MESH,
        )

    near = [(dg, dz) for dz in range(samp_size) for dg in (-1, 0, 1) if (dg, dz) != (0, 0)]
    far = [(dg, 0) for dg in range(2, gene_size - 1)]
    barrier = pltpu.get_barrier_semaphore()
    for dg, dz in near + far:
        pl.semaphore_signal(
            barrier, inc=1, device_id=there(dg, dz), device_id_type=pl.DeviceIdType.MESH
        )
    pl.semaphore_wait(barrier, len(near + far))

    pending = []
    for dg, dz in near:
        copy = send(
            message_ref,
            arrived.at[1 - dg, z],
            message_send.at[1 - dg, dz],
            message_recv.at[1 - dg, z],
            there(dg, dz),
        )
        copy.start()
        pending.append(copy)
    arrived[1, z] = message_ref[...]

    ones = jnp.ones((16, samp_dev), jnp.bfloat16)
    step = 256 if var_dev % 256 == 0 else var_dev
    for v in range(0, var_dev, step):
        part = dosage_ref[v : v + step, :]
        wide = part.astype(jnp.float32)
        square = wide * wide
        upper = square.astype(jnp.bfloat16)
        lower = (square - upper.astype(jnp.float32)).astype(jnp.bfloat16)
        moments[z, 0:8, v : v + step] = rows_dot(ones, part)[0:8]
        moments[z, 8:16, v : v + step] = (rows_dot(ones, upper) + rows_dot(ones, lower))[0:8]
    for dz in range(1, samp_size):
        copy = send(
            moments.at[z], moments.at[z], moment_send.at[dz], moment_recv.at[z], there(0, dz)
        )
        copy.start()
        pending.append(copy)

    for r in (0, 1, 2):
        for dz in range(samp_size):
            if (r, dz) != (1, 0):
                source = lax.rem(z + dz, samp_size)
                send(
                    message_ref,
                    arrived.at[r, source],
                    message_send.at[r, dz],
                    message_recv.at[r, source],
                    there(0, 1),
                ).wait_recv()

    alone[...] = jnp.zeros_like(alone)
    sums, codings = [], []
    for r in range(3):
        for pair in range(gene_dev // 2):
            codes = [[], []]
            for half in range(2):
                j = 2 * pair + half
                blocks = [arrived[r, k, j, 0:across, :] for k in range(samp_size)]
                mean = whole_sum(sum(blocks)) / samples
                spread = whole_sum(sum(jnp.square(k - mean) for k in blocks)) / samples
                factor = lax.rsqrt(spread + epsilon)
                total = jnp.zeros((across, LANES), jnp.float32)
                power = jnp.zeros((across, LANES), jnp.float32)
                for k in range(samp_size):
                    value = ((blocks[k] - mean) * factor).astype(jnp.bfloat16).astype(jnp.float32)
                    total = total + value
                    power = power + value * value
                    if r == 1:
                        codes[half].append(encode(value))
                sums.append(whole_sum(total))
                power = whole_sum(power) + 1e-30
                inverse = lax.rsqrt(power)
                codings.append((32000.0 * inverse, power * inverse / 32000.0))
                own = (arrived[r, z, j, 0:across, :] - mean) * factor
                own = own.astype(jnp.bfloat16).astype(jnp.float32)
                row = r * gene_dev + j
                for h in range(across):
                    alone[row : row + 1, h * LANES : (h + 1) * LANES] = own[h : h + 1, :]
            if r == 1:
                for k in range(samp_size):
                    table[pair, k, 0:across, :] = codes[0][k] + (codes[1][k] << 16)

    each = alone[...].astype(jnp.bfloat16)
    for v in range(0, var_dev, step):
        directs[z, :, v : v + step] = rows_dot(each, dosage_ref[v : v + step, :])
    for dz in range(1, samp_size):
        copy = send(
            directs.at[z], directs.at[z], direct_send.at[dz], direct_recv.at[z], there(0, dz)
        )
        copy.start()
        pending.append(copy)

    for dz in range(1, samp_size):
        source = lax.rem(z + dz, samp_size)
        send(
            moments.at[z],
            moments.at[source],
            moment_send.at[dz],
            moment_recv.at[source],
            there(0, dz),
        ).wait_recv()
    totals = sum(moments[k, 0:1, :] for k in range(samp_size))
    squares = sum(moments[k, 8:9, :] for k in range(samp_size))
    row_mean = totals / samples
    row_scale = lax.rsqrt((squares / samples - row_mean * row_mean + epsilon) * samples)

    power = powers()
    words = table.shape[0]

    height = gene_dev * share

    def gather(k):
        first = pl.multiple_of(lax.rem(z + 1 + k, samp_size) * share, share)

        def tile(t, carry):
            p = pl.multiple_of((t // across) * 16, 16)
            s = pl.multiple_of((t % across) * LANES, LANES)
            index = perms_ref[pl.ds(pl.multiple_of(first + p, 16), 16), pl.ds(s, LANES)]
            low = index & (LANES - 1)
            high = index >> 7
            found = [jnp.zeros(index.shape, jnp.int32) for _ in range(words)]
            for c in range(samp_size):
                for h in range(across):
                    here = high == c * across + h
                    for w in range(words):
                        entry = jnp.broadcast_to(table[w, c, h : h + 1, :], index.shape)
                        found[w] = jnp.where(here, pick(entry, low), found[w])
            for w in range(words):
                for half in range(2):
                    row = pl.multiple_of(height + (2 * w + half) * share + p, 16)
                    shuffled[k, pl.ds(row, 16), pl.ds(s, LANES)] = decode(
                        found[w] >> (16 * half), power
                    )
            return carry

        lax.fori_loop(0, share // 16 * across, tile, 0)

    def shift(k, right):
        side = 1 if right else 0
        slot = 0 if right else 2
        return send(
            shuffled.at[k, pl.ds(height, height)],
            shuffled.at[k, pl.ds(slot * height, height)],
            shift_send.at[side, k],
            shift_recv.at[side, k],
            there(1 if right else -1, 0),
        )

    has_left, has_right = g > 0, g < gene_size - 1

    def give(k):
        pl.when(has_right)(lambda: shift(k, True).start())
        pl.when(has_left)(lambda: shift(k, False).start())

    def take(k):
        pl.when(has_left)(lambda: shift(k, True).wait_recv())
        pl.when(has_right)(lambda: shift(k, False).wait_recv())

    def spent(k, carry):
        pl.when(has_right)(lambda: shift(k, True).wait_send())
        pl.when(has_left)(lambda: shift(k, False).wait_send())
        return carry

    def clear(slot):
        for k in range(samp_size):
            shuffled[k, slot * height : (slot + 1) * height, :] = jnp.zeros(
                (height, samp_dev), jnp.bfloat16
            )

    pl.when(jnp.logical_not(has_left))(lambda: clear(0))
    pl.when(jnp.logical_not(has_right))(lambda: clear(2))

    def multiply(k):
        take(k)
        taken = shuffled[k]
        column = jnp.sum(taken.astype(jnp.float32), axis=1, keepdims=True)
        for v in range(0, var_dev, step):
            centred = (
                rows_dot(taken, dosage_ref[v : v + step, :]) - column * row_mean[:, v : v + step]
            ) * row_scale[:, v : v + step]
            for row in range(genes):
                rows = slice(row * share, (row + 1) * share)
                mine[rows, v : v + step] = centred[rows, :] * codings[row][0]

    def remote(k):
        multiply(k)
        outgoing[k] = jnp.round(mine[...]).astype(jnp.int32).astype(jnp.int16)
        send(
            outgoing.at[k],
            incoming.at[k],
            block_send.at[k],
            block_recv.at[k],
            {"gene": g, "samp": lax.rem(z + 1 + k, samp_size)},
        ).start()

    gather(0)
    give(0)

    def turn(k, carry):
        gather(k + 1)
        give(k + 1)
        remote(k)
        return carry

    lax.fori_loop(0, samp_size - 1, turn, 0)
    multiply(samp_size - 1)

    for dz in range(1, samp_size):
        source = lax.rem(z + dz, samp_size)
        send(
            directs.at[z],
            directs.at[source],
            direct_send.at[dz],
            direct_recv.at[source],
            there(0, dz),
        ).wait_recv()
    direct = sum(directs[k] for k in range(samp_size))
    place = (g * var_dev + lax.broadcasted_iota(jnp.int32, (1, var_dev), 1)).astype(jnp.float32)
    peaks[...] = jnp.zeros_like(peaks)
    for k in range(samp_size - 1):
        send(
            outgoing.at[k], incoming.at[k], block_send.at[k], block_recv.at[k], there(0, k + 1)
        ).wait()

    def fold(values):
        best = values[:, 0:LANES]
        for t in range(LANES, var_dev, LANES):
            best = jnp.maximum(best, values[:, t : t + LANES])
        return best

    for row in range(genes):
        r, j = row // gene_dev, row % gene_dev
        start = arrived[r, 0, j, across : across + 1, 0:1]
        finish = arrived[r, 0, j, across + 1 : across + 2, 0:1]
        inside = (place >= start) & (place < finish)
        weight = jnp.where(inside, row_scale, 0.0)
        rows = slice(row * share, (row + 1) * share)
        total = mine[rows, :] + row_mean * row_scale * (sums[row] * codings[row][0])
        for k in range(samp_size - 1):
            total = total + incoming[k, rows, :].astype(jnp.int32).astype(jnp.float32)
        peaks[rows, :] = fold(jnp.where(inside, jnp.abs(total), 0.0)) * codings[row][1]
        last = genes * share + row
        peaks[last : last + 1, :] = fold(jnp.abs(direct[row : row + 1, :]) * weight)
    rows_z[z] = jnp.max(peaks[...].T, axis=0, keepdims=True)
    for dz in range(1, samp_size):
        copy = send(rows_z.at[z], rows_z.at[z], row_send.at[dz], row_recv.at[z], there(0, dz))
        copy.start()
        pending.append(copy)
    for dz in range(1, samp_size):
        source = lax.rem(z + dz, samp_size)
        send(
            rows_z.at[z], rows_z.at[source], row_send.at[dz], row_recv.at[source], there(0, dz)
        ).wait_recv()
    for dg in range(1, gene_size):
        copy = send(rows_z, out_ref.at[g], all_send.at[dg], all_recv.at[g], there(dg, 0))
        copy.start()
        pending.append(copy)
    out_ref[g] = rows_z[...]
    for dg in range(1, gene_size):
        source = lax.rem(g + dg, gene_size)
        send(
            rows_z, out_ref.at[source], all_send.at[dg], all_recv.at[source], there(dg, 0)
        ).wait_recv()
    for copy in pending:
        copy.wait_send()
    lax.fori_loop(0, samp_size, spent, 0)


def up_to(size, unit):
    return -(-size // unit) * unit


def scan(dosage, expression, perms, windows):
    var_dev, samp_dev = dosage.shape
    gene_dev = expression.shape[1]
    permutations = perms.shape[0]
    gene_size, samp_size = lax.axis_size("gene"), lax.axis_size("samp")
    genes = 3 * gene_dev
    across = samp_dev // LANES
    share = permutations // samp_size
    height = up_to(across + 2, 8)
    lines = jnp.concatenate(
        [
            expression.T.reshape(gene_dev, across, LANES),
            jnp.broadcast_to(
                windows.astype(jnp.float32)[:, :, None], (gene_dev, 2, LANES)
            ),
            jnp.zeros((gene_dev, height - across - 2, LANES), jnp.float32),
        ],
        axis=1,
    )
    width = up_to(genes * share + genes, LANES)
    few = up_to(genes, 16)
    dma = pltpu.SemaphoreType.DMA
    kernel = functools.partial(scan_kernel, gene_size, samp_size, samp_dev * samp_size)
    return pl.pallas_call(
        kernel,
        out_shape=jax.ShapeDtypeStruct((gene_size, samp_size, 1, width), jnp.float32),
        in_specs=[pl.BlockSpec(memory_space=pltpu.VMEM)] * 3,
        out_specs=pl.BlockSpec(memory_space=pltpu.VMEM),
        scratch_shapes=[
            pltpu.VMEM((3, samp_size, gene_dev, height, LANES), jnp.float32),
            pltpu.VMEM((gene_dev // 2, samp_size, up_to(across, 8), LANES), jnp.int32),
            pltpu.VMEM((few, samp_dev), jnp.float32),
            pltpu.VMEM((samp_size, 16, var_dev), jnp.float32),
            pltpu.VMEM((samp_size, few, var_dev), jnp.float32),
            pltpu.VMEM((samp_size, genes * share, samp_dev), jnp.bfloat16),
            pltpu.VMEM((genes * share, var_dev), jnp.float32),
            pltpu.VMEM((samp_size - 1, genes * share, var_dev), jnp.int16),
            pltpu.VMEM((samp_size - 1, genes * share, var_dev), jnp.int16),
            pltpu.VMEM((width, LANES), jnp.float32),
            pltpu.VMEM((samp_size, 1, width), jnp.float32),
            dma((3, samp_size)),
            dma((3, samp_size)),
        ]
        + [dma((samp_size,))] * 8
        + [dma((gene_size,))] * 2
        + [dma((2, samp_size))] * 2,
        compiler_params=pltpu.CompilerParams(
            collective_id=0, has_side_effects=True, vmem_limit_bytes=48 * 2**20
        ),
    )(lines, dosage, perms)


def on_device(dosage, expression, perms, windows, order):
    gene_dev = expression.shape[1]
    permutations = perms.shape[0]
    gene_size, samp_size = lax.axis_size("gene"), lax.axis_size("samp")
    gene_place = lax.axis_index("gene")
    share = permutations // samp_size
    genes = 3 * gene_dev
    found = scan(dosage, expression, perms, windows)[:, :, 0, :]
    maxima = found[:, :, : genes * share].reshape(gene_size, samp_size, 3, gene_dev, share)
    maxima = maxima.transpose(0, 2, 3, 1, 4).reshape(gene_size, 3, gene_dev, permutations)
    seen = found[:, 0, genes * share : genes * share + genes].reshape(gene_size, 3, gene_dev, 1)
    every = jnp.concatenate([maxima, seen], axis=3)
    every = jnp.maximum(
        every[:, 1],
        jnp.maximum(jnp.roll(every[:, 0], -1, axis=0), jnp.roll(every[:, 2], 1, axis=0)),
    )
    observed = lax.dynamic_slice_in_dim(every[:, :, permutations], gene_place, 1, 0)[0]
    ranked = every[:, :, :permutations].reshape(gene_size * gene_dev, permutations)
    ids = jnp.arange(order.shape[0], dtype=jnp.int32)
    rank = jnp.sum(jnp.where(order[None, :] == ids[:, None], ids[None, :], 0), axis=1)
    mine = gene_place * gene_dev + jnp.arange(gene_dev, dtype=jnp.int32)
    later = rank[None, :] >= mine[:, None]
    successive = jnp.max(jnp.where(later[:, :, None], ranked[None], 0.0), axis=1)
    return (observed, successive)


def solution(mesh):
    placed = (P("gene", "samp"), P("samp", "gene"), P(None, "samp"), P("gene", None), P())
    return jax.shard_map(
        on_device,
        mesh=mesh,
        in_specs=placed,
        out_specs=(P("gene"), P("gene", None)),
        check_vma=False,
    )
```

```python
import functools

import jax
import jax.numpy as jnp
from jax import lax
from jax.experimental import pallas as pl
from jax.experimental.pallas import tpu as pltpu
from jax.sharding import PartitionSpec as P

epsilon = 1e-06


LANES = 128


def encode(value):
    size = jnp.abs(value)
    down = jnp.zeros(value.shape, jnp.int32)
    for step in (64, 32, 16, 8, 4, 2, 1):
        small = size < 2.0 ** (7 - step)
        size = jnp.where(small, size * 2.0**step, size)
        down = down + jnp.where(small, step, 0)
    mantissa = jnp.where(value < 0, -2.0 * size, 2.0 * size).astype(jnp.int32)
    return down * 512 + mantissa + 256


def powers():
    lane = lax.broadcasted_iota(jnp.int32, (16, LANES), 1)
    power = jnp.full((16, LANES), 0.5, jnp.float32)
    for step in (64, 32, 16, 8, 4, 2, 1):
        power = jnp.where((lane & step) != 0, power * 2.0**-step, power)
    return jnp.where(lane >= 126, 0.0, power)


def pick(table, index):
    return jnp.take_along_axis(table, index, axis=1)


def decode(code, power):
    mantissa = ((code & 511) - 256).astype(jnp.float32)
    return (mantissa * pick(power, (code >> 9) & 127)).astype(jnp.bfloat16)


def rows_dot(left, right):
    return lax.dot_general(left, right, (((1,), (1,)), ((), ())), preferred_element_type=jnp.float32)


def whole_sum(block):
    return jnp.sum(jnp.sum(block, axis=0, keepdims=True), axis=1, keepdims=True)


def scan_kernel(
    gene_size,
    samp_size,
    samples,
    message_ref,
    dosage_ref,
    perms_ref,
    out_ref,
    arrived,
    table,
    alone,
    moments,
    directs,
    shuffled,
    mine,
    outgoing,
    incoming,
    peaks,
    rows_z,
    message_send,
    message_recv,
    moment_send,
    moment_recv,
    direct_send,
    direct_recv,
    block_send,
    block_recv,
    row_send,
    row_recv,
    all_send,
    all_recv,
    shift_send,
    shift_recv,
):
    var_dev, samp_dev = dosage_ref.shape
    permutations = perms_ref.shape[0]
    gene_dev = message_ref.shape[0]
    genes = 3 * gene_dev
    share = permutations // samp_size
    across = samp_dev // LANES
    g = lax.axis_index("gene")
    z = lax.axis_index("samp")

    def there(dg, dz):
        return {
            "gene": lax.rem(g + dg + gene_size, gene_size),
            "samp": lax.rem(z + dz, samp_size),
        }

    def send(source, target, send_sem, recv_sem, device):
        return pltpu.make_async_remote_copy(
            src_ref=source,
            dst_ref=target,
            send_sem=send_sem,
            recv_sem=recv_sem,
            device_id=device,
            device_id_type=pl.DeviceIdType.MESH,
        )

    near = [(dg, dz) for dz in range(samp_size) for dg in (-1, 0, 1) if (dg, dz) != (0, 0)]
    far = [(dg, 0) for dg in range(2, gene_size - 1)]
    barrier = pltpu.get_barrier_semaphore()
    for dg, dz in near + far:
        pl.semaphore_signal(
            barrier, inc=1, device_id=there(dg, dz), device_id_type=pl.DeviceIdType.MESH
        )
    pl.semaphore_wait(barrier, len(near + far))

    pending = []
    for dg, dz in near:
        copy = send(
            message_ref,
            arrived.at[1 - dg, z],
            message_send.at[1 - dg, dz],
            message_recv.at[1 - dg, z],
            there(dg, dz),
        )
        copy.start()
        pending.append(copy)
    arrived[1, z] = message_ref[...]

    ones = jnp.ones((16, samp_dev), jnp.bfloat16)
    step = 256 if var_dev % 256 == 0 else var_dev
    for v in range(0, var_dev, step):
        part = dosage_ref[v : v + step, :]
        wide = part.astype(jnp.float32)
        square = wide * wide
        upper = square.astype(jnp.bfloat16)
        lower = (square - upper.astype(jnp.float32)).astype(jnp.bfloat16)
        moments[z, 0:8, v : v + step] = rows_dot(ones, part)[0:8]
        moments[z, 8:16, v : v + step] = (rows_dot(ones, upper) + rows_dot(ones, lower))[0:8]
    for dz in range(1, samp_size):
        copy = send(
            moments.at[z], moments.at[z], moment_send.at[dz], moment_recv.at[z], there(0, dz)
        )
        copy.start()
        pending.append(copy)

    for r in (0, 1, 2):
        for dz in range(samp_size):
            if (r, dz) != (1, 0):
                source = lax.rem(z + dz, samp_size)
                send(
                    message_ref,
                    arrived.at[r, source],
                    message_send.at[r, dz],
                    message_recv.at[r, source],
                    there(0, 1),
                ).wait_recv()

    alone[...] = jnp.zeros_like(alone)
    sums, codings = [], []
    for r in range(3):
        for pair in range(gene_dev // 2):
            codes = [[], []]
            for half in range(2):
                j = 2 * pair + half
                blocks = [arrived[r, k, j, 0:across, :] for k in range(samp_size)]
                mean = whole_sum(sum(blocks)) / samples
                spread = whole_sum(sum(jnp.square(k - mean) for k in blocks)) / samples
                factor = lax.rsqrt(spread + epsilon)
                total = jnp.zeros((across, LANES), jnp.float32)
                power = jnp.zeros((across, LANES), jnp.float32)
                for k in range(samp_size):
                    value = ((blocks[k] - mean) * factor).astype(jnp.bfloat16).astype(jnp.float32)
                    total = total + value
                    power = power + value * value
                    if r == 1:
                        codes[half].append(encode(value))
                sums.append(whole_sum(total))
                power = whole_sum(power) + 1e-30
                inverse = lax.rsqrt(power)
                codings.append((32000.0 * inverse, power * inverse / 32000.0))
                own = (arrived[r, z, j, 0:across, :] - mean) * factor
                own = own.astype(jnp.bfloat16).astype(jnp.float32)
                row = r * gene_dev + j
                for h in range(across):
                    alone[row : row + 1, h * LANES : (h + 1) * LANES] = own[h : h + 1, :]
            if r == 1:
                for k in range(samp_size):
                    table[pair, k, 0:across, :] = codes[0][k] + (codes[1][k] << 16)

    each = alone[...].astype(jnp.bfloat16)
    for v in range(0, var_dev, step):
        directs[z, :, v : v + step] = rows_dot(each, dosage_ref[v : v + step, :])
    for dz in range(1, samp_size):
        copy = send(
            directs.at[z], directs.at[z], direct_send.at[dz], direct_recv.at[z], there(0, dz)
        )
        copy.start()
        pending.append(copy)

    for dz in range(1, samp_size):
        source = lax.rem(z + dz, samp_size)
        send(
            moments.at[z],
            moments.at[source],
            moment_send.at[dz],
            moment_recv.at[source],
            there(0, dz),
        ).wait_recv()
    totals = sum(moments[k, 0:1, :] for k in range(samp_size))
    squares = sum(moments[k, 8:9, :] for k in range(samp_size))
    row_mean = totals / samples
    row_scale = lax.rsqrt((squares / samples - row_mean * row_mean + epsilon) * samples)

    power = powers()
    words = table.shape[0]

    height = gene_dev * share

    def gather(k):
        first = pl.multiple_of(lax.rem(z + 1 + k, samp_size) * share, share)

        def tile(t, carry):
            p = pl.multiple_of((t // across) * 16, 16)
            s = pl.multiple_of((t % across) * LANES, LANES)
            index = perms_ref[pl.ds(pl.multiple_of(first + p, 16), 16), pl.ds(s, LANES)]
            parts = []
            for part in (index[0:8], index[8:16]):
                low = part & (LANES - 1)
                high = part >> 7
                picked = [jnp.zeros(part.shape, jnp.int32) for _ in range(words)]
                for c in range(samp_size):
                    for h in range(across):
                        here = high == c * across + h
                        for w in range(words):
                            entry = jnp.broadcast_to(table[w, c, h : h + 1, :], part.shape)
                            picked[w] = jnp.where(here, pick(entry, low), picked[w])
                parts.append(picked)
            found = [jnp.concatenate(pair, axis=0) for pair in zip(*parts)]
            for w in range(words):
                for half in range(2):
                    row = pl.multiple_of(height + (2 * w + half) * share + p, 16)
                    shuffled[k, pl.ds(row, 16), pl.ds(s, LANES)] = decode(
                        found[w] >> (16 * half), power
                    )
            return carry

        lax.fori_loop(0, share // 16 * across, tile, 0)

    def shift(k, right):
        side = 1 if right else 0
        slot = 0 if right else 2
        return send(
            shuffled.at[k, pl.ds(height, height)],
            shuffled.at[k, pl.ds(slot * height, height)],
            shift_send.at[side, k],
            shift_recv.at[side, k],
            there(1 if right else -1, 0),
        )

    has_left, has_right = g > 0, g < gene_size - 1

    def give(k):
        pl.when(has_right)(lambda: shift(k, True).start())
        pl.when(has_left)(lambda: shift(k, False).start())

    def take(k):
        pl.when(has_left)(lambda: shift(k, True).wait_recv())
        pl.when(has_right)(lambda: shift(k, False).wait_recv())

    def spent(k, carry):
        pl.when(has_right)(lambda: shift(k, True).wait_send())
        pl.when(has_left)(lambda: shift(k, False).wait_send())
        return carry

    def clear(slot):
        for k in range(samp_size):
            shuffled[k, slot * height : (slot + 1) * height, :] = jnp.zeros(
                (height, samp_dev), jnp.bfloat16
            )

    pl.when(jnp.logical_not(has_left))(lambda: clear(0))
    pl.when(jnp.logical_not(has_right))(lambda: clear(2))

    def multiply(k):
        take(k)
        taken = shuffled[k]
        column = jnp.sum(taken.astype(jnp.float32), axis=1, keepdims=True)
        for v in range(0, var_dev, step):
            centred = (
                rows_dot(taken, dosage_ref[v : v + step, :]) - column * row_mean[:, v : v + step]
            ) * row_scale[:, v : v + step]
            for row in range(genes):
                rows = slice(row * share, (row + 1) * share)
                mine[rows, v : v + step] = centred[rows, :] * codings[row][0]

    def remote(k):
        multiply(k)
        outgoing[k] = jnp.round(mine[...]).astype(jnp.int32).astype(jnp.int16)
        send(
            outgoing.at[k],
            incoming.at[k],
            block_send.at[k],
            block_recv.at[k],
            {"gene": g, "samp": lax.rem(z + 1 + k, samp_size)},
        ).start()

    gather(0)
    give(0)

    def turn(k, carry):
        gather(k + 1)
        give(k + 1)
        remote(k)
        return carry

    lax.fori_loop(0, samp_size - 1, turn, 0)
    multiply(samp_size - 1)

    for dz in range(1, samp_size):
        source = lax.rem(z + dz, samp_size)
        send(
            directs.at[z],
            directs.at[source],
            direct_send.at[dz],
            direct_recv.at[source],
            there(0, dz),
        ).wait_recv()
    direct = sum(directs[k] for k in range(samp_size))
    place = (g * var_dev + lax.broadcasted_iota(jnp.int32, (1, var_dev), 1)).astype(jnp.float32)
    peaks[...] = jnp.zeros_like(peaks)
    for k in range(samp_size - 1):
        send(
            outgoing.at[k], incoming.at[k], block_send.at[k], block_recv.at[k], there(0, k + 1)
        ).wait()

    def fold(values):
        best = values[:, 0:LANES]
        for t in range(LANES, var_dev, LANES):
            best = jnp.maximum(best, values[:, t : t + LANES])
        return best

    for row in range(genes):
        r, j = row // gene_dev, row % gene_dev
        start = arrived[r, 0, j, across : across + 1, 0:1]
        finish = arrived[r, 0, j, across + 1 : across + 2, 0:1]
        inside = (place >= start) & (place < finish)
        weight = jnp.where(inside, row_scale, 0.0)
        rows = slice(row * share, (row + 1) * share)
        total = mine[rows, :] + row_mean * row_scale * (sums[row] * codings[row][0])
        for k in range(samp_size - 1):
            total = total + incoming[k, rows, :].astype(jnp.int32).astype(jnp.float32)
        peaks[rows, :] = fold(jnp.where(inside, jnp.abs(total), 0.0)) * codings[row][1]
        last = genes * share + row
        peaks[last : last + 1, :] = fold(jnp.abs(direct[row : row + 1, :]) * weight)
    rows_z[z] = jnp.max(peaks[...].T, axis=0, keepdims=True)
    for dz in range(1, samp_size):
        copy = send(rows_z.at[z], rows_z.at[z], row_send.at[dz], row_recv.at[z], there(0, dz))
        copy.start()
        pending.append(copy)
    for dz in range(1, samp_size):
        source = lax.rem(z + dz, samp_size)
        send(
            rows_z.at[z], rows_z.at[source], row_send.at[dz], row_recv.at[source], there(0, dz)
        ).wait_recv()
    for dg in range(1, gene_size):
        copy = send(rows_z, out_ref.at[g], all_send.at[dg], all_recv.at[g], there(dg, 0))
        copy.start()
        pending.append(copy)
    out_ref[g] = rows_z[...]
    for dg in range(1, gene_size):
        source = lax.rem(g + dg, gene_size)
        send(
            rows_z, out_ref.at[source], all_send.at[dg], all_recv.at[source], there(dg, 0)
        ).wait_recv()
    for copy in pending:
        copy.wait_send()
    lax.fori_loop(0, samp_size, spent, 0)


def up_to(size, unit):
    return -(-size // unit) * unit


def scan(dosage, expression, perms, windows):
    var_dev, samp_dev = dosage.shape
    gene_dev = expression.shape[1]
    permutations = perms.shape[0]
    gene_size, samp_size = lax.axis_size("gene"), lax.axis_size("samp")
    genes = 3 * gene_dev
    across = samp_dev // LANES
    share = permutations // samp_size
    height = up_to(across + 2, 8)
    lines = jnp.concatenate(
        [
            expression.T.reshape(gene_dev, across, LANES),
            jnp.broadcast_to(
                windows.astype(jnp.float32)[:, :, None], (gene_dev, 2, LANES)
            ),
            jnp.zeros((gene_dev, height - across - 2, LANES), jnp.float32),
        ],
        axis=1,
    )
    width = up_to(genes * share + genes, LANES)
    few = up_to(genes, 16)
    dma = pltpu.SemaphoreType.DMA
    kernel = functools.partial(scan_kernel, gene_size, samp_size, samp_dev * samp_size)
    return pl.pallas_call(
        kernel,
        out_shape=jax.ShapeDtypeStruct((gene_size, samp_size, 1, width), jnp.float32),
        in_specs=[pl.BlockSpec(memory_space=pltpu.VMEM)] * 3,
        out_specs=pl.BlockSpec(memory_space=pltpu.VMEM),
        scratch_shapes=[
            pltpu.VMEM((3, samp_size, gene_dev, height, LANES), jnp.float32),
            pltpu.VMEM((gene_dev // 2, samp_size, up_to(across, 8), LANES), jnp.int32),
            pltpu.VMEM((few, samp_dev), jnp.float32),
            pltpu.VMEM((samp_size, 16, var_dev), jnp.float32),
            pltpu.VMEM((samp_size, few, var_dev), jnp.float32),
            pltpu.VMEM((samp_size, genes * share, samp_dev), jnp.bfloat16),
            pltpu.VMEM((genes * share, var_dev), jnp.float32),
            pltpu.VMEM((samp_size - 1, genes * share, var_dev), jnp.int16),
            pltpu.VMEM((samp_size - 1, genes * share, var_dev), jnp.int16),
            pltpu.VMEM((width, LANES), jnp.float32),
            pltpu.VMEM((samp_size, 1, width), jnp.float32),
            dma((3, samp_size)),
            dma((3, samp_size)),
        ]
        + [dma((samp_size,))] * 8
        + [dma((gene_size,))] * 2
        + [dma((2, samp_size))] * 2,
        compiler_params=pltpu.CompilerParams(
            collective_id=0, has_side_effects=True, vmem_limit_bytes=48 * 2**20
        ),
    )(lines, dosage, perms)


def on_device(dosage, expression, perms, windows, order):
    gene_dev = expression.shape[1]
    permutations = perms.shape[0]
    gene_size, samp_size = lax.axis_size("gene"), lax.axis_size("samp")
    gene_place = lax.axis_index("gene")
    share = permutations // samp_size
    genes = 3 * gene_dev
    found = scan(dosage, expression, perms, windows)[:, :, 0, :]
    maxima = found[:, :, : genes * share].reshape(gene_size, samp_size, 3, gene_dev, share)
    maxima = maxima.transpose(0, 2, 3, 1, 4).reshape(gene_size, 3, gene_dev, permutations)
    seen = found[:, 0, genes * share : genes * share + genes].reshape(gene_size, 3, gene_dev, 1)
    every = jnp.concatenate([maxima, seen], axis=3)
    every = jnp.maximum(
        every[:, 1],
        jnp.maximum(jnp.roll(every[:, 0], -1, axis=0), jnp.roll(every[:, 2], 1, axis=0)),
    )
    observed = lax.dynamic_slice_in_dim(every[:, :, permutations], gene_place, 1, 0)[0]
    ranked = every[:, :, :permutations].reshape(gene_size * gene_dev, permutations)
    ids = jnp.arange(order.shape[0], dtype=jnp.int32)
    rank = jnp.sum(jnp.where(order[None, :] == ids[:, None], ids[None, :], 0), axis=1)
    mine = gene_place * gene_dev + jnp.arange(gene_dev, dtype=jnp.int32)
    later = rank[None, :] >= mine[:, None]
    successive = jnp.max(jnp.where(later[:, :, None], ranked[None], 0.0), axis=1)
    return (observed, successive)


def solution(mesh):
    placed = (P("gene", "samp"), P("samp", "gene"), P(None, "samp"), P("gene", None), P())
    return jax.shard_map(
        on_device,
        mesh=mesh,
        in_specs=placed,
        out_specs=(P("gene"), P("gene", None)),
        check_vma=False,
    )
```

```python
import functools

import jax
import jax.numpy as jnp
from jax import lax
from jax.experimental import pallas as pl
from jax.experimental.pallas import tpu as pltpu
from jax.sharding import PartitionSpec as P

epsilon = 1e-06


LANES = 128


def encode(value):
    size = jnp.abs(value)
    down = jnp.zeros(value.shape, jnp.int32)
    for step in (64, 32, 16, 8, 4, 2, 1):
        small = size < 2.0 ** (7 - step)
        size = jnp.where(small, size * 2.0**step, size)
        down = down + jnp.where(small, step, 0)
    mantissa = jnp.where(value < 0, -2.0 * size, 2.0 * size).astype(jnp.int32)
    return down * 512 + mantissa + 256


def powers():
    lane = lax.broadcasted_iota(jnp.int32, (16, LANES), 1)
    power = jnp.full((16, LANES), 0.5, jnp.float32)
    for step in (64, 32, 16, 8, 4, 2, 1):
        power = jnp.where((lane & step) != 0, power * 2.0**-step, power)
    return jnp.where(lane >= 126, 0.0, power)


def pick(table, index):
    return jnp.take_along_axis(table, index, axis=1)


def decode(code, power):
    mantissa = ((code & 511) - 256).astype(jnp.float32)
    return (mantissa * pick(power, (code >> 9) & 127)).astype(jnp.bfloat16)


def rows_dot(left, right):
    return lax.dot_general(left, right, (((1,), (1,)), ((), ())), preferred_element_type=jnp.float32)


def whole_sum(block):
    return jnp.sum(jnp.sum(block, axis=0, keepdims=True), axis=1, keepdims=True)


def scan_kernel(
    gene_size,
    samp_size,
    samples,
    message_ref,
    dosage_ref,
    perms_ref,
    out_ref,
    arrived,
    table,
    alone,
    moments,
    directs,
    shuffled,
    mine,
    outgoing,
    incoming,
    peaks,
    rows_z,
    message_send,
    message_recv,
    moment_send,
    moment_recv,
    direct_send,
    direct_recv,
    block_send,
    block_recv,
    row_send,
    row_recv,
    all_send,
    all_recv,
):
    var_dev, samp_dev = dosage_ref.shape
    permutations = perms_ref.shape[0]
    gene_dev = message_ref.shape[0]
    genes = 3 * gene_dev
    share = permutations // samp_size
    across = samp_dev // LANES
    g = lax.axis_index("gene")
    z = lax.axis_index("samp")

    def there(dg, dz):
        return {
            "gene": lax.rem(g + dg + gene_size, gene_size),
            "samp": lax.rem(z + dz, samp_size),
        }

    def send(source, target, send_sem, recv_sem, device):
        return pltpu.make_async_remote_copy(
            src_ref=source,
            dst_ref=target,
            send_sem=send_sem,
            recv_sem=recv_sem,
            device_id=device,
            device_id_type=pl.DeviceIdType.MESH,
        )

    near = [(dg, dz) for dz in range(samp_size) for dg in (-1, 0, 1) if (dg, dz) != (0, 0)]
    far = [(dg, 0) for dg in range(2, gene_size - 1)]
    barrier = pltpu.get_barrier_semaphore()
    for dg, dz in near + far:
        pl.semaphore_signal(
            barrier, inc=1, device_id=there(dg, dz), device_id_type=pl.DeviceIdType.MESH
        )
    pl.semaphore_wait(barrier, len(near + far))

    pending = []
    for dg, dz in near:
        copy = send(
            message_ref,
            arrived.at[1 - dg, z],
            message_send.at[1 - dg, dz],
            message_recv.at[1 - dg, z],
            there(dg, dz),
        )
        copy.start()
        pending.append(copy)
    arrived[1, z] = message_ref[...]

    ones = jnp.ones((16, samp_dev), jnp.bfloat16)
    step = 256 if var_dev % 256 == 0 else var_dev
    for v in range(0, var_dev, step):
        part = dosage_ref[v : v + step, :]
        wide = part.astype(jnp.float32)
        square = wide * wide
        upper = square.astype(jnp.bfloat16)
        lower = (square - upper.astype(jnp.float32)).astype(jnp.bfloat16)
        moments[z, 0:8, v : v + step] = rows_dot(ones, part)[0:8]
        moments[z, 8:16, v : v + step] = (rows_dot(ones, upper) + rows_dot(ones, lower))[0:8]
    for dz in range(1, samp_size):
        copy = send(
            moments.at[z], moments.at[z], moment_send.at[dz], moment_recv.at[z], there(0, dz)
        )
        copy.start()
        pending.append(copy)

    for r in (0, 1, 2):
        for dz in range(samp_size):
            if (r, dz) != (1, 0):
                source = lax.rem(z + dz, samp_size)
                send(
                    message_ref,
                    arrived.at[r, source],
                    message_send.at[r, dz],
                    message_recv.at[r, source],
                    there(0, 1),
                ).wait_recv()

    alone[...] = jnp.zeros_like(alone)
    sums, codings = [], []
    for r in range(3):
        for pair in range(gene_dev // 2):
            codes = [[], []]
            for half in range(2):
                j = 2 * pair + half
                blocks = [arrived[r, k, j, 0:across, :] for k in range(samp_size)]
                mean = whole_sum(sum(blocks)) / samples
                spread = whole_sum(sum(jnp.square(k - mean) for k in blocks)) / samples
                factor = lax.rsqrt(spread + epsilon)
                total = jnp.zeros((across, LANES), jnp.float32)
                power = jnp.zeros((across, LANES), jnp.float32)
                for k in range(samp_size):
                    value = ((blocks[k] - mean) * factor).astype(jnp.bfloat16).astype(jnp.float32)
                    total = total + value
                    power = power + value * value
                    codes[half].append(encode(value))
                sums.append(whole_sum(total))
                power = whole_sum(power) + 1e-30
                inverse = lax.rsqrt(power)
                codings.append((32000.0 * inverse, power * inverse / 32000.0))
                own = (arrived[r, z, j, 0:across, :] - mean) * factor
                own = own.astype(jnp.bfloat16).astype(jnp.float32)
                row = r * gene_dev + j
                for h in range(across):
                    alone[row : row + 1, h * LANES : (h + 1) * LANES] = own[h : h + 1, :]
            word = r * (gene_dev // 2) + pair
            for k in range(samp_size):
                table[word, k, 0:across, :] = codes[0][k] + (codes[1][k] << 16)

    each = alone[...].astype(jnp.bfloat16)
    for v in range(0, var_dev, step):
        directs[z, :, v : v + step] = rows_dot(each, dosage_ref[v : v + step, :])
    for dz in range(1, samp_size):
        copy = send(
            directs.at[z], directs.at[z], direct_send.at[dz], direct_recv.at[z], there(0, dz)
        )
        copy.start()
        pending.append(copy)

    for dz in range(1, samp_size):
        source = lax.rem(z + dz, samp_size)
        send(
            moments.at[z],
            moments.at[source],
            moment_send.at[dz],
            moment_recv.at[source],
            there(0, dz),
        ).wait_recv()
    totals = sum(moments[k, 0:1, :] for k in range(samp_size))
    squares = sum(moments[k, 8:9, :] for k in range(samp_size))
    row_mean = totals / samples
    row_scale = lax.rsqrt((squares / samples - row_mean * row_mean + epsilon) * samples)

    power = powers()
    words = table.shape[0]

    def gather(k):
        first = pl.multiple_of(lax.rem(z + 1 + k, samp_size) * share, share)

        def tile(t, carry):
            p = pl.multiple_of((t // across) * 16, 16)
            s = pl.multiple_of((t % across) * LANES, LANES)
            index = perms_ref[pl.ds(pl.multiple_of(first + p, 16), 16), pl.ds(s, LANES)]
            parts = []
            for part in (index[0:8], index[8:16]):
                low = part & (LANES - 1)
                high = part >> 7
                picked = [jnp.zeros(part.shape, jnp.int32) for _ in range(words)]
                for c in range(samp_size):
                    for h in range(across):
                        here = high == c * across + h
                        for w in range(words):
                            entry = jnp.broadcast_to(table[w, c, h : h + 1, :], part.shape)
                            picked[w] = jnp.where(here, pick(entry, low), picked[w])
                parts.append(picked)
            found = [jnp.concatenate(pair, axis=0) for pair in zip(*parts)]
            for w in range(words):
                for half in range(2):
                    row = pl.multiple_of((2 * w + half) * share + p, 16)
                    shuffled[k, pl.ds(row, 16), pl.ds(s, LANES)] = decode(
                        found[w] >> (16 * half), power
                    )
            return carry

        lax.fori_loop(0, share // 16 * across, tile, 0)

    def multiply(k):
        taken = shuffled[k]
        column = jnp.sum(taken.astype(jnp.float32), axis=1, keepdims=True)
        for v in range(0, var_dev, step):
            centred = (
                rows_dot(taken, dosage_ref[v : v + step, :]) - column * row_mean[:, v : v + step]
            ) * row_scale[:, v : v + step]
            for row in range(genes):
                rows = slice(row * share, (row + 1) * share)
                mine[rows, v : v + step] = centred[rows, :] * codings[row][0]

    def remote(k):
        multiply(k)
        outgoing[k] = jnp.round(mine[...]).astype(jnp.int32).astype(jnp.int16)
        send(
            outgoing.at[k],
            incoming.at[k],
            block_send.at[k],
            block_recv.at[k],
            {"gene": g, "samp": lax.rem(z + 1 + k, samp_size)},
        ).start()

    def turn(k, carry):
        gather(k)
        remote(k)
        return carry

    lax.fori_loop(0, samp_size - 1, turn, 0)
    gather(samp_size - 1)
    multiply(samp_size - 1)

    for dz in range(1, samp_size):
        source = lax.rem(z + dz, samp_size)
        send(
            directs.at[z],
            directs.at[source],
            direct_send.at[dz],
            direct_recv.at[source],
            there(0, dz),
        ).wait_recv()
    direct = sum(directs[k] for k in range(samp_size))
    place = (g * var_dev + lax.broadcasted_iota(jnp.int32, (1, var_dev), 1)).astype(jnp.float32)
    peaks[...] = jnp.zeros_like(peaks)
    for k in range(samp_size - 1):
        send(
            outgoing.at[k], incoming.at[k], block_send.at[k], block_recv.at[k], there(0, k + 1)
        ).wait()

    def fold(values):
        best = values[:, 0:LANES]
        for t in range(LANES, var_dev, LANES):
            best = jnp.maximum(best, values[:, t : t + LANES])
        return best

    for row in range(genes):
        r, j = row // gene_dev, row % gene_dev
        start = arrived[r, 0, j, across : across + 1, 0:1]
        finish = arrived[r, 0, j, across + 1 : across + 2, 0:1]
        inside = (place >= start) & (place < finish)
        weight = jnp.where(inside, row_scale, 0.0)
        rows = slice(row * share, (row + 1) * share)
        total = mine[rows, :] + row_mean * row_scale * (sums[row] * codings[row][0])
        for k in range(samp_size - 1):
            total = total + incoming[k, rows, :].astype(jnp.int32).astype(jnp.float32)
        peaks[rows, :] = fold(jnp.where(inside, jnp.abs(total), 0.0)) * codings[row][1]
        last = genes * share + row
        peaks[last : last + 1, :] = fold(jnp.abs(direct[row : row + 1, :]) * weight)
    rows_z[z] = jnp.max(peaks[...].T, axis=0, keepdims=True)
    for dz in range(1, samp_size):
        copy = send(rows_z.at[z], rows_z.at[z], row_send.at[dz], row_recv.at[z], there(0, dz))
        copy.start()
        pending.append(copy)
    for dz in range(1, samp_size):
        source = lax.rem(z + dz, samp_size)
        send(
            rows_z.at[z], rows_z.at[source], row_send.at[dz], row_recv.at[source], there(0, dz)
        ).wait_recv()
    for dg in range(1, gene_size):
        copy = send(rows_z, out_ref.at[g], all_send.at[dg], all_recv.at[g], there(dg, 0))
        copy.start()
        pending.append(copy)
    out_ref[g] = rows_z[...]
    for dg in range(1, gene_size):
        source = lax.rem(g + dg, gene_size)
        send(
            rows_z, out_ref.at[source], all_send.at[dg], all_recv.at[source], there(dg, 0)
        ).wait_recv()
    for copy in pending:
        copy.wait_send()


def up_to(size, unit):
    return -(-size // unit) * unit


def scan(dosage, expression, perms, windows):
    var_dev, samp_dev = dosage.shape
    gene_dev = expression.shape[1]
    permutations = perms.shape[0]
    gene_size, samp_size = lax.axis_size("gene"), lax.axis_size("samp")
    genes = 3 * gene_dev
    across = samp_dev // LANES
    share = permutations // samp_size
    height = up_to(across + 2, 8)
    lines = jnp.concatenate(
        [
            expression.T.reshape(gene_dev, across, LANES),
            jnp.broadcast_to(
                windows.astype(jnp.float32)[:, :, None], (gene_dev, 2, LANES)
            ),
            jnp.zeros((gene_dev, height - across - 2, LANES), jnp.float32),
        ],
        axis=1,
    )
    width = up_to(genes * share + genes, LANES)
    few = up_to(genes, 16)
    dma = pltpu.SemaphoreType.DMA
    kernel = functools.partial(scan_kernel, gene_size, samp_size, samp_dev * samp_size)
    return pl.pallas_call(
        kernel,
        out_shape=jax.ShapeDtypeStruct((gene_size, samp_size, 1, width), jnp.float32),
        in_specs=[pl.BlockSpec(memory_space=pltpu.VMEM)] * 3,
        out_specs=pl.BlockSpec(memory_space=pltpu.VMEM),
        scratch_shapes=[
            pltpu.VMEM((3, samp_size, gene_dev, height, LANES), jnp.float32),
            pltpu.VMEM((genes // 2, samp_size, up_to(across, 8), LANES), jnp.int32),
            pltpu.VMEM((few, samp_dev), jnp.float32),
            pltpu.VMEM((samp_size, 16, var_dev), jnp.float32),
            pltpu.VMEM((samp_size, few, var_dev), jnp.float32),
            pltpu.VMEM((samp_size, genes * share, samp_dev), jnp.bfloat16),
            pltpu.VMEM((genes * share, var_dev), jnp.float32),
            pltpu.VMEM((samp_size - 1, genes * share, var_dev), jnp.int16),
            pltpu.VMEM((samp_size - 1, genes * share, var_dev), jnp.int16),
            pltpu.VMEM((width, LANES), jnp.float32),
            pltpu.VMEM((samp_size, 1, width), jnp.float32),
            dma((3, samp_size)),
            dma((3, samp_size)),
        ]
        + [dma((samp_size,))] * 8
        + [dma((gene_size,))] * 2,
        compiler_params=pltpu.CompilerParams(
            collective_id=0, has_side_effects=True, vmem_limit_bytes=48 * 2**20
        ),
    )(lines, dosage, perms)


def on_device(dosage, expression, perms, windows, order):
    gene_dev = expression.shape[1]
    permutations = perms.shape[0]
    gene_size, samp_size = lax.axis_size("gene"), lax.axis_size("samp")
    gene_place = lax.axis_index("gene")
    share = permutations // samp_size
    genes = 3 * gene_dev
    found = scan(dosage, expression, perms, windows)[:, :, 0, :]
    maxima = found[:, :, : genes * share].reshape(gene_size, samp_size, 3, gene_dev, share)
    maxima = maxima.transpose(0, 2, 3, 1, 4).reshape(gene_size, 3, gene_dev, permutations)
    seen = found[:, 0, genes * share : genes * share + genes].reshape(gene_size, 3, gene_dev, 1)
    every = jnp.concatenate([maxima, seen], axis=3)
    every = jnp.maximum(
        every[:, 1],
        jnp.maximum(jnp.roll(every[:, 0], -1, axis=0), jnp.roll(every[:, 2], 1, axis=0)),
    )
    observed = lax.dynamic_slice_in_dim(every[:, :, permutations], gene_place, 1, 0)[0]
    ranked = every[:, :, :permutations].reshape(gene_size * gene_dev, permutations)
    ids = jnp.arange(order.shape[0], dtype=jnp.int32)
    rank = jnp.sum(jnp.where(order[None, :] == ids[:, None], ids[None, :], 0), axis=1)
    mine = gene_place * gene_dev + jnp.arange(gene_dev, dtype=jnp.int32)
    later = rank[None, :] >= mine[:, None]
    successive = jnp.max(jnp.where(later[:, :, None], ranked[None], 0.0), axis=1)
    return (observed, successive)


def solution(mesh):
    placed = (P("gene", "samp"), P("samp", "gene"), P(None, "samp"), P("gene", None), P())
    return jax.shard_map(
        on_device,
        mesh=mesh,
        in_specs=placed,
        out_specs=(P("gene"), P("gene", None)),
        check_vma=False,
    )
```
